256 devices in a mesh: seq: 32 (over x, y, core), tp: 8 (over z).
Axes of the slice: x: 4, y: 4, z: 8, core: 2. Of those that a mesh axis runs over, the one named last changes fastest.
Arguments:
- tokens: bfloat16 [65536, 16384], P('seq', 'tp'), may hold values from -120 to 120
- sketch: float32 [16384, 256], P('tp'), may hold values from -0.046875 to 0.046875
Outputs:
- basis: float32 [65536, 256], P('seq')
- coefficients: float32 [256, 16384], P('seq', 'tp')
The draws below stay inside these ranges and needn't reach their ends.
All inputs are finite; a program needn't handle non-finite values.
Results may differ from the reference program's by a relative error of at most 0.0003.
Values sent between devices are 32-bit elements; how exact they have to be, the bound alone decides.
A program may use at most 64 MiB of HBM per device.

```python
import math
import jax
import jax.numpy as jnp
from jax import lax

D = 16384
K = 256
TOK_DEV = 2048
TOKENS = 65536
N_SEQ = 32


def draw_tokens(key, part):
    key = jax.random.fold_in(key, 11)
    key_a, key_b, key_c = jax.random.split(key, 3)
    values = jnp.clip(jax.random.normal(key_a, (TOKENS, D), jnp.float32), -4.0, 4.0)
    row_scale = jnp.exp(jax.random.uniform(key_b, (TOKENS, 1), jnp.float32, 0.0, math.log(10.0)))
    col_scale = jnp.exp(jax.random.uniform(key_c, (1, D), jnp.float32, 0.0, math.log(10.0)))
    position = jnp.arange(TOKENS, dtype=jnp.float32) / (TOKENS - 1)
    trend = jnp.exp(position * math.log(3.0))[:, None]
    return (values * row_scale * col_scale * trend * 0.1).astype(jnp.bfloat16)


def levels(rng, extent, cuts, low, high):
    factor_of, own = 1.0, jax.random.fold_in(rng, 6)
    for dim, parts in cuts:
        heights = jnp.exp(jax.random.uniform(jax.random.fold_in(own, dim), (parts,), jnp.float32, low / len(cuts), high / len(cuts)))
        factor_of = factor_of * jnp.repeat(heights, extent[dim] // parts).reshape([-1 if axis == dim else 1 for axis in range(len(extent))])
    return factor_of


def centred(own_key, dims, spread, most, shards=(), held_as=jnp.bfloat16):
    result = spread * jax.random.normal(own_key, dims, jnp.float32)
    if shards:
        result = result * levels(own_key, dims, shards, -0.22, 0.18)
    return jnp.clip(result, -most, most).astype(held_as)


def setup_inputs(seed: int = 0) -> dict:
    key_of = jax.random.split(jax.random.key(seed), 3)
    tokens = draw_tokens(jax.random.fold_in(key_of[2], 71), 0)
    sketch = centred(key_of[1], (D, K), D ** -0.5, 0.046875, ((0, 8),), jnp.float32)
    return {"tokens": tokens, "sketch": sketch}


def split_parts(matrix):
    high = matrix.astype(jnp.bfloat16)
    kept = lax.optimization_barrier(high)
    low = (matrix - kept.astype(matrix.dtype)).astype(jnp.bfloat16)
    return (high, low)

def reference(tokens, sketch):
    blocks = tokens.reshape(N_SEQ, TOK_DEV, D)
    sketch_high, sketch_low = split_parts(sketch)

    def project(block):
        first = jnp.dot(block.astype(jnp.float32), sketch_high.astype(jnp.float32), preferred_element_type=jnp.float32)
        return first + jnp.dot(block.astype(jnp.float32), sketch_low.astype(jnp.float32), preferred_element_type=jnp.float32)
    sketched = lax.map(project, blocks).reshape(TOKENS, K)
    gram = jnp.dot(sketched.T.astype(jnp.float32), sketched.astype(jnp.float32), precision=lax.Precision.HIGHEST, preferred_element_type=jnp.float32)
    lower = jnp.linalg.cholesky(gram)
    basis_t = jax.scipy.linalg.solve_triangular(lower, sketched.T, lower=True) * math.sqrt(TOKENS)
    basis_high, basis_low = split_parts(basis_t)

    def accumulate(index, total):
        start = (index * TOK_DEV).astype(jnp.int32)
        left_high = lax.dynamic_slice_in_dim(basis_high, start, TOK_DEV, 1)
        left_low = lax.dynamic_slice_in_dim(basis_low, start, TOK_DEV, 1)
        right = lax.dynamic_slice_in_dim(tokens, start, TOK_DEV, 0)
        term = jnp.dot(left_high.astype(jnp.float32), right.astype(jnp.float32), preferred_element_type=jnp.float32)
        term = term + jnp.dot(left_low.astype(jnp.float32), right.astype(jnp.float32), preferred_element_type=jnp.float32)
        return total + term
    summed = lax.fori_loop(0, N_SEQ, accumulate, jnp.zeros((K, D), jnp.float32))
    return (basis_t.T, summed / TOKENS)
```

```python
import functools
import math

import jax
import jax.numpy as jnp
from jax import lax
from jax.experimental import pallas as pl
from jax.experimental.pallas import tpu as pltpu
from jax.sharding import PartitionSpec as P

MESH = pl.DeviceIdType.MESH
HIGHEST = lax.Precision.HIGHEST
F32 = jnp.float32
BF16 = jnp.bfloat16
HALF = 128
PANEL = 8


def dot32(a, b, dims):
    return lax.dot_general(a, b, (dims, ((), ())), precision=HIGHEST, preferred_element_type=F32)


def nn(a, b):
    return dot32(a, b, ((1,), (0,)))


def nt(a, b):
    return dot32(a, b, ((1,), (1,)))


def tn(a, b):
    return dot32(a, b, ((0,), (0,)))


def split_parts(value):
    high = value.astype(BF16)
    low = (value - high.astype(F32)).astype(BF16)
    return high, low


def inverse_factor(matrix):
    size = matrix.shape[0]
    sub = lax.broadcasted_iota(jnp.int32, (PANEL, HALF), 0)
    lane = lax.broadcasted_iota(jnp.int32, (PANEL, HALF), 1)
    rest = matrix
    done = []
    for first in range(0, size, PANEL):
        panel = rest[:PANEL]
        below = rest[PANEL:]
        columns = [
            jnp.broadcast_to(panel[:, first + j : first + j + 1], (PANEL, HALF)) for j in range(PANEL)
        ]
        inside = (lane >= first) & (lane < first + PANEL)
        panel = jnp.where(inside, jnp.where(lane - first == sub, 1.0, 0.0), panel)
        work = columns + [panel]
        kept = jnp.zeros((PANEL, HALF), F32)
        pivots = jnp.ones((PANEL, HALF), F32)
        for j in range(PANEL):
            here = sub == j
            rows = [jnp.broadcast_to(item[j : j + 1], (PANEL, HALF)) for item in work]
            pivot = rows[0]
            factor = jnp.where(here, -1.0, work[0]) * (1.0 / pivot)
            kept = jnp.where(here, rows[-1], kept)
            pivots = jnp.where(here, pivot, pivots)
            work = [
                jnp.where(here, 0.0, item) - factor * row for item, row in zip(work[1:], rows[1:])
            ]
        scaled = kept * lax.rsqrt(pivots)
        done.append(jnp.where(lane <= sub + first, scaled, 0.0))
        if first + PANEL < size:
            solved = work[0]
            count = size - first - PANEL
            below_lane = lax.broadcasted_iota(jnp.int32, (count, HALF), 1)
            update = jnp.where((below_lane >= first) & (below_lane < first + PANEL), 0.0, below)
            for j in range(PANEL):
                update = update - below[:, first + j : first + j + 1] * solved[j : j + 1]
            rest = update
        yield None
    return jnp.concatenate(done, axis=0)


def kernel(
    nq, nz, total,
    tok_hbm, sk_hbm, basis_out, coef_out,
    tok, sk, weights, part, ring, s_all,
    gsrc0, gsrc1, ga0, ga1, gb0, gb1, gfull0, gfull1,
    c0, cx, cp, cr, cg, outs, landed, basis_v,
    tok_sem, sk_sem, rs_send, rs_recv, ag_send, ag_recv, g_send, g_recv,
    c_send, c_recv, out_sem,
):
    rows, feats = tok.shape
    chunk = rows // nz
    unit = chunk // 2
    dist = nz // 2
    me = lax.axis_index("seq")
    z = lax.axis_index("tp")
    q, core = me // 2, lax.rem(me, 2)
    other = q * 2 + (1 - core)
    up, down = lax.rem(z + 1, nz), lax.rem(z + nz - 1, nz)
    members = 2 * nz
    mine = z * 2 + core

    def remote(src, dst, send, recv, seq_id, z_id):
        return pltpu.make_async_remote_copy(
            src_ref=src, dst_ref=dst, send_sem=send, recv_sem=recv,
            device_id=(seq_id, z_id), device_id_type=MESH,
        )

    def xy_peer(o):
        peer = lax.rem(q + o, nq)
        return peer, peer * 2 + core

    def zc_peer(o):
        peer = lax.rem(mine + o, members)
        return q * 2 + lax.rem(peer, 2), peer // 2

    def chunk_of(j):
        return lax.rem(z + j, nz)

    sk_copies = [
        pltpu.make_async_copy(sk_hbm.at[:, pl.ds(h * HALF, HALF)], sk.at[h], sk_sem.at[h])
        for h in range(2)
    ]
    tok_copies = {}
    order = [dist]
    for s in range(1, dist):
        order += [dist - s, nz - dist + s]
    order.append(0)
    for j in order:
        at = pl.ds(pl.multiple_of(chunk_of(j) * chunk, chunk), chunk)
        tok_copies[j] = pltpu.make_async_copy(tok_hbm.at[at], tok.at[at], tok_sem.at[j])
    sk_copies[0].start()
    tok_copies[order[0]].start()
    sk_copies[1].start()
    for j in order[1:]:
        tok_copies[j].start()

    barrier = pltpu.get_barrier_semaphore()

    def greet_xy(o, carry):
        _, seq_id = xy_peer(o)
        pl.semaphore_signal(barrier, inc=1, device_id=(seq_id, z), device_id_type=MESH)
        return carry

    def greet_zc(o, carry):
        seq_id, z_id = zc_peer(o)
        pl.semaphore_signal(barrier, inc=1, device_id=(seq_id, z_id), device_id_type=MESH)
        return carry

    lax.fori_loop(1, nq, greet_xy, 0)
    lax.fori_loop(1, members, greet_zc, 0)

    loaded = set()

    def prepare_weights(h):
        sk_copies[h].wait()
        step = min(256, feats)

        @pl.loop(0, feats // step)
        def _(i):
            at = pl.ds(pl.multiple_of(i * step, step), step)
            high, low = split_parts(sk[h, at, :])
            weights[h, at, :HALF] = high
            weights[h, at, HALF:] = low

    def compute_part(h, j):
        if j not in loaded:
            tok_copies[j].wait()
            loaded.add(j)
        at = pl.ds(pl.multiple_of(chunk_of(j) * chunk, chunk), chunk)
        both = jnp.dot(tok[at, :], weights[h], preferred_element_type=F32)
        part[h, j] = both[:, :HALF] + both[:, HALF:]

    def unit_rows(u):
        return pl.ds(u * unit, unit)

    sent = []

    def rs_copy(h, d, s, u, src):
        slot = s * 2 + u
        return remote(
            src, ring.at[h, d, slot], rs_send.at[h, d, slot], rs_recv.at[h, d, slot],
            me, up if d == 0 else down,
        )

    def rs_send_unit(h, d, s, u, src):
        copy = rs_copy(h, d, s, u, src)
        copy.start()
        sent.append(copy)

    def rs_wait(h, d, s, u):
        rs_copy(h, d, s, u, ring.at[h, d, s * 2 + u]).wait_recv()

    def reduce_scatter(h):
        prepare_weights(h)
        compute_part(h, dist)
        if h == 0:
            pl.semaphore_wait(barrier, nq - 1 + members - 1)
        for d in range(2):
            rs_send_unit(h, d, 0, d, part.at[h, dist, unit_rows(d)])
        yield
        for s in range(1, dist):
            places = (dist - s, nz - dist + s)
            for j in places:
                compute_part(h, j)
            if s == 1:
                for d in range(2):
                    u = 1 - d
                    rs_send_unit(h, d, 1, u, part.at[h, places[d], unit_rows(u)])
            yield
            for u_step in ([1] if s == 1 else [0, 1]):
                for d in range(2):
                    u = (1 - d) if u_step == 0 else d
                    rs_wait(h, d, s - 1, u)
                    slot = (s - 1) * 2 + u
                    ring[h, d, slot] = ring[h, d, slot] + part[h, places[d], unit_rows(u), :]
                    rs_send_unit(h, d, s, u, ring.at[h, d, slot])
            yield
        compute_part(h, 0)
        yield
        for u in range(2):
            for d in range(2):
                rs_wait(h, d, dist - 1, u) if (dist > 1 or u == d) else None
        at = pl.multiple_of(z * chunk, chunk)
        for u in range(2):
            slot = (dist - 1) * 2 + u
            value = part[h, 0, unit_rows(u), :] + ring[h, 0, slot] + ring[h, 1, slot]
            s_all[h, pl.ds(at + u * unit, unit), :] = value
        yield

    def ag_copy(h, d, k, u):
        c = lax.rem(z + nz - k, nz) if d == 0 else lax.rem(z + k, nz)
        at = pl.ds(pl.multiple_of(c * chunk + u * unit, unit), unit)
        slot = k * 2 + u
        return remote(
            s_all.at[h, at], s_all.at[h, at], ag_send.at[h, d, slot], ag_recv.at[h, d, slot],
            me, up if d == 0 else down,
        )

    def ag_arrived(h, d, k, u):
        c = lax.rem(z + nz - k - 1, nz) if d == 0 else lax.rem(z + k + 1, nz)
        at = pl.ds(pl.multiple_of(c * chunk + u * unit, unit), unit)
        slot = k * 2 + u
        remote(
            s_all.at[h, at], s_all.at[h, at], ag_send.at[h, d, slot], ag_recv.at[h, d, slot],
            me, up if d == 0 else down,
        ).wait_recv()

    def all_gather(h):
        for k in range(dist):
            for step in range(2):
                for d in range(2):
                    u = d if step == 0 else 1 - d
                    if k > 0:
                        ag_arrived(h, d, k - 1, u)
                    if k < dist - 1 or step == 0:
                        copy = ag_copy(h, d, k, u)
                        copy.start()
                        sent.append(copy)
            yield
        for d in range(2):
            ag_arrived(h, d, dist - 1, d)
        yield

    def spread(g, step, count, start_one, sized):
        def body(o, carry):
            start_one(o).start()
            return carry

        lax.fori_loop(1, count, body, 0)

        def wait_all():
            probe = remote(sized, sized, g_send.at[g, step], g_recv.at[g, step], me, up)
            probe.wait_recv()
            probe.wait_send()

        return wait_all

    def gram_sum(g, src, ga, gb, full):
        piece = src.shape[0] // nq

        def rows_of(i):
            return pl.ds(pl.multiple_of(i * piece, piece), piece)

        def first(o):
            peer, seq_id = xy_peer(o)
            return remote(
                src.at[rows_of(peer)], ga.at[q], g_send.at[g, 0], g_recv.at[g, 0], seq_id, z
            )

        wait_first = spread(g, 0, nq, first, ga.at[pl.ds(0, nq - 1)])
        ga[q] = src[rows_of(q), :]
        yield
        wait_first()
        value = ga[0]
        for i in range(1, nq):
            value = value + ga[i]
        gb[mine] = value

        def second(o):
            seq_id, z_id = zc_peer(o)
            return remote(gb.at[mine], gb.at[mine], g_send.at[g, 1], g_recv.at[g, 1], seq_id, z_id)

        wait_second = spread(g, 1, members, second, gb.at[pl.ds(0, members - 1)])
        yield
        wait_second()
        value = gb[0]
        for i in range(1, members):
            value = value + gb[i]
        full[rows_of(q), :] = value

        def third(o):
            _, seq_id = xy_peer(o)
            return remote(
                full.at[rows_of(q)], full.at[rows_of(q)], g_send.at[g, 2], g_recv.at[g, 2],
                seq_id, z,
            )

        wait_third = spread(g, 2, nq, third, full.at[pl.ds(0, (nq - 1) * piece)])
        yield
        wait_third()
        yield

    tile = min(512, feats)
    per_tile = tile // HALF

    def product(h, j, first, after_tile=None):
        at = pl.ds(pl.multiple_of(chunk_of(j) * chunk, chunk), chunk)
        high, low = split_parts(s_all[h, at, :].T)
        left = jnp.concatenate([high, low], axis=0)
        for t in range(feats // tile):
            both = jnp.dot(left, tok[at, t * tile : (t + 1) * tile], preferred_element_type=F32)
            value = both[:HALF] + both[HALF:]
            for i in range(per_tile):
                item = value[:, i * HALF : (i + 1) * HALF]
                p = t * per_tile + i
                c0[h, p] = item if first else c0[h, p] + item
            if after_tile is not None:
                after_tile(t)

    split = HALF // 2

    def core_copy(h, t):
        give = pl.ds(pl.multiple_of((1 - core) * split, split), split)
        at = pl.ds(t * per_tile, per_tile)
        return remote(
            c0.at[h, at, give], cx.at[h, at], c_send.at[h, t], c_recv.at[h, t], other, z
        )

    tiles = feats // tile

    def start_core(h):
        def after(t):
            copy = core_copy(h, t)
            copy.start()
            sent.append(copy)

        return after

    def coef_sum(h):
        keep = pl.ds(pl.multiple_of(core * split, split), split)
        for t in range(tiles):
            core_copy(h, t).wait_recv()
            for i in range(per_tile):
                p = t * per_tile + i
                cp[h, p] = c0[h, p, keep, :] + cx[h, p]

        def body(o, carry):
            peer, seq_id = xy_peer(o)
            remote(
                cp.at[h, peer], cr.at[h, q], c_send.at[h, tiles], c_recv.at[h, tiles], seq_id, z
            ).start()
            return carry

        lax.fori_loop(1, nq, body, 0)
        cr[h, q] = cp[h, q]
        yield
        sized = cr.at[h, pl.ds(0, nq - 1)]
        probe = remote(sized, sized, c_send.at[h, tiles], c_recv.at[h, tiles], me, up)
        probe.wait_recv()
        probe.wait_send()
        value = cr[h, 0]
        for i in range(1, nq):
            value = value + cr[h, i]
        cg[h, keep, :] = value
        copy = remote(
            cg.at[h, keep], cg.at[h, keep], c_send.at[h, tiles + 1], c_recv.at[h, tiles + 1],
            other, z,
        )
        copy.start()
        yield
        copy.wait()
        yield

    def run(gen, steps=None):
        count = 0
        while steps is None or count < steps:
            try:
                next(gen)
            except StopIteration as stop:
                return stop.value
            count += 1
        return None

    rs = [reduce_scatter(h) for h in range(2)]
    ag = [all_gather(h) for h in range(2)]
    coef = [coef_sum(h) for h in range(2)]
    rs_steps = 1 + 2 * (dist - 1)

    run(rs[0], rs_steps + 1)
    run(rs[1], 2)
    run(rs[0], 1)
    own = pl.ds(pl.multiple_of(z * chunk, chunk), chunk)
    own0 = s_all[0, own, :]
    gsrc0[...] = tn(own0, own0)
    gram0 = gram_sum(0, gsrc0, ga0, gb0, gfull0)
    run(gram0, 1)
    run(rs[1], 1)
    run(gram0, 1)
    run(rs[1], rs_steps - 3)
    run(ag[0], 1)
    run(gram0, 1)
    run(rs[1], 1)
    run(rs[1], 1)
    own1 = s_all[1, own, :]
    gsrc1[:HALF] = tn(own1, s_all[0, own, :])
    gsrc1[HALF:] = tn(own1, own1)
    gram1 = gram_sum(1, gsrc1, ga1, gb1, gfull1)
    run(gram1, 1)
    run(gram0, 1)
    chol0 = inverse_factor(gfull0[...])
    run(chol0, 3)
    run(gram1, 1)
    run(ag[0], 1)
    run(chol0, 4)
    run(gram1, 1)
    run(chol0, 3)
    run(ag[0], 1)
    w00 = run(chol0)
    run(gram1)
    low10 = nt(gfull1[:HALF], w00)
    run(ag[0], dist - 3 if dist > 3 else 0)
    run(ag[1], 1)
    schur = gfull1[HALF:] - nt(low10, low10)
    chol1 = inverse_factor(schur)
    run(chol1, 4)
    run(ag[0])
    run(chol1, 2)
    for i, j in enumerate(order):
        product(0, j, i == 0, start_core(0) if i == nz - 1 else None)
    run(ag[1], 1)
    run(chol1, 4)
    run(coef[0], 1)
    run(ag[1], 1)
    mixed = nn(low10, w00)
    w11 = run(chol1)
    run(ag[1], 1)
    w10 = -nn(w11, mixed)
    run(coef[0], 1)
    late = [dist]
    if dist > 1:
        late = [dist - 1, nz - dist + 1, dist]
    early = [j for j in order if j not in late]
    for i, j in enumerate(early):
        product(1, j, i == 0)
    run(ag[1])
    run(coef[0])
    for i, j in enumerate(late):
        last = i == len(late) - 1
        product(1, j, not early and i == 0, start_core(1) if last else None)
    run(coef[1], 1)

    root = math.sqrt(total)
    b00, b10, b11 = w00 * root, w10 * root, w11 * root
    basis_copies = []
    step = min(256, rows)
    for i in range(rows // step):
        at = pl.ds(i * step, step)
        left0, left1 = s_all[0, at, :], s_all[1, at, :]
        basis_v[at, :HALF] = nt(left0, b00)
        basis_v[at, HALF:] = nt(left0, b10) + nt(left1, b11)
        copy = pltpu.make_async_copy(basis_v.at[at], basis_out.at[at], out_sem.at[i])
        copy.start()
        basis_copies.append(copy)

    run(coef[1])
    block = 2 * HALF // (2 * nq)
    outs[:HALF] = nn(w00, cg[0]) / root
    outs[HALF:] = (nn(w10, cg[0]) + nn(w11, cg[1])) / root

    def rows_for(seq_id):
        return pl.ds(pl.multiple_of(seq_id * block, block), block)

    def last_hop(o, carry):
        _, seq_id = xy_peer(o)
        remote(
            outs.at[rows_for(seq_id)], landed.at[q], c_send.at[2, 0], c_recv.at[2, 0], seq_id, z
        ).start()
        return carry

    lax.fori_loop(1, nq, last_hop, 0)
    landed[q] = outs[rows_for(me), :]
    sized = landed.at[pl.ds(0, nq - 1)]
    probe = remote(sized, sized, c_send.at[2, 0], c_recv.at[2, 0], me, up)
    probe.wait_recv()
    probe.wait_send()
    for i in range(nq):
        coef_out[:, i * HALF : (i + 1) * HALF] = landed[i]

    for copy in sent:
        copy.wait_send()
    for copy in basis_copies:
        copy.wait()


def shards(mesh_shape, tokens, sketch):
    rows, feats = tokens.shape
    seq, nz = mesh_shape["seq"], mesh_shape["tp"]
    nq = seq // 2
    total = rows * seq
    chunk = rows // nz
    unit = chunk // 2
    dist = nz // 2
    k = 2 * HALF
    dma = pltpu.SemaphoreType.DMA
    tiles = feats // min(512, feats)
    return pl.pallas_call(
        functools.partial(kernel, nq, nz, total),
        out_shape=(
            jax.ShapeDtypeStruct((rows, k), F32),
            jax.ShapeDtypeStruct((k // seq, feats), F32),
        ),
        in_specs=[pl.BlockSpec(memory_space=pl.ANY)] * 2,
        out_specs=(pl.BlockSpec(memory_space=pl.ANY), pl.BlockSpec(memory_space=pltpu.VMEM)),
        scratch_shapes=[
            pltpu.VMEM((rows, feats), BF16),
            pltpu.VMEM((2, feats, HALF), F32),
            pltpu.VMEM((2, feats, k), BF16),
            pltpu.VMEM((2, nz, chunk, HALF), F32),
            pltpu.VMEM((2, 2, nz, unit, HALF), F32),
            pltpu.VMEM((2, rows, HALF), F32),
            pltpu.VMEM((HALF, HALF), F32),
            pltpu.VMEM((k, HALF), F32),
            pltpu.VMEM((nq, HALF // nq, HALF), F32),
            pltpu.VMEM((nq, k // nq, HALF), F32),
            pltpu.VMEM((2 * nz, HALF // nq, HALF), F32),
            pltpu.VMEM((2 * nz, k // nq, HALF), F32),
            pltpu.VMEM((HALF, HALF), F32),
            pltpu.VMEM((k, HALF), F32),
            pltpu.VMEM((2, nq, HALF, HALF), F32),
            pltpu.VMEM((2, nq, HALF // 2, HALF), F32),
            pltpu.VMEM((2, nq, HALF // 2, HALF), F32),
            pltpu.VMEM((2, nq, HALF // 2, HALF), F32),
            pltpu.VMEM((2, HALF, HALF), F32),
            pltpu.VMEM((k, HALF), F32),
            pltpu.VMEM((nq, k // seq, HALF), F32),
            pltpu.VMEM((rows, k), F32),
            dma((nz,)),
            dma((2,)),
            dma((2, 2, nz)),
            dma((2, 2, nz)),
            dma((2, 2, nz)),
            dma((2, 2, nz)),
            dma((2, 3)),
            dma((2, 3)),
            dma((3, tiles + 2)),
            dma((3, tiles + 2)),
            dma((max(1, rows // 256),)),
        ],
        compiler_params=pltpu.CompilerParams(
            collective_id=0, has_side_effects=True, vmem_limit_bytes=50 * 1024 * 1024
        ),
    )(tokens, sketch)


def solution(mesh):
    return jax.shard_map(
        functools.partial(shards, dict(mesh.shape)),
        mesh=mesh,
        in_specs=(P("seq", "tp"), P("tp", None)),
        out_specs=(P("seq", None), P("seq", "tp")),
        check_vma=False,
    )
```

```python
import functools
import math

import jax
import jax.numpy as jnp
from jax import lax
from jax.experimental import pallas as pl
from jax.experimental.pallas import tpu as pltpu
from jax.sharding import PartitionSpec as P

MESH = pl.DeviceIdType.MESH
HIGHEST = lax.Precision.HIGHEST
F32 = jnp.float32
BF16 = jnp.bfloat16
HALF = 128
PANEL = 8


def dot32(a, b, dims):
    return lax.dot_general(a, b, (dims, ((), ())), precision=HIGHEST, preferred_element_type=F32)


def nn(a, b):
    return dot32(a, b, ((1,), (0,)))


def nt(a, b):
    return dot32(a, b, ((1,), (1,)))


def tn(a, b):
    return dot32(a, b, ((0,), (0,)))


def split_parts(value):
    high = value.astype(BF16)
    low = (value - high.astype(F32)).astype(BF16)
    return high, low


def inverse_factor(matrix):
    size = matrix.shape[0]
    sub = lax.broadcasted_iota(jnp.int32, (PANEL, HALF), 0)
    lane = lax.broadcasted_iota(jnp.int32, (PANEL, HALF), 1)
    rest = matrix
    done = []
    for first in range(0, size, PANEL):
        panel = rest[:PANEL]
        below = rest[PANEL:]
        columns = [
            jnp.broadcast_to(panel[:, first + j : first + j + 1], (PANEL, HALF)) for j in range(PANEL)
        ]
        inside = (lane >= first) & (lane < first + PANEL)
        panel = jnp.where(inside, jnp.where(lane - first == sub, 1.0, 0.0), panel)
        work = columns + [panel]
        kept = jnp.zeros((PANEL, HALF), F32)
        pivots = jnp.ones((PANEL, HALF), F32)
        for j in range(PANEL):
            here = sub == j
            rows = [jnp.broadcast_to(item[j : j + 1], (PANEL, HALF)) for item in work]
            pivot = rows[0]
            factor = jnp.where(here, -1.0, work[0]) * (1.0 / pivot)
            kept = jnp.where(here, rows[-1], kept)
            pivots = jnp.where(here, pivot, pivots)
            work = [
                jnp.where(here, 0.0, item) - factor * row for item, row in zip(work[1:], rows[1:])
            ]
        scaled = kept * lax.rsqrt(pivots)
        done.append(jnp.where(lane <= sub + first, scaled, 0.0))
        if first + PANEL < size:
            solved = work[0]
            count = size - first - PANEL
            below_lane = lax.broadcasted_iota(jnp.int32, (count, HALF), 1)
            update = jnp.where((below_lane >= first) & (below_lane < first + PANEL), 0.0, below)
            for j in range(PANEL):
                update = update - below[:, first + j : first + j + 1] * solved[j : j + 1]
            rest = update
        yield None
    return jnp.concatenate(done, axis=0)


def kernel(
    nq, nz, total,
    tok_hbm, sk_hbm, basis_out, coef_out,
    tok, sk, weights, part, ring, s_all,
    gsrc, ga, gb, gfull,
    c0, cx, cp, cr, cg, outs, landed,
    tok_sem, sk_sem, rs_send, rs_recv, ag_send, ag_recv, g_send, g_recv,
    c_send, c_recv,
):
    rows, feats = tok.shape
    chunk = rows // nz
    unit = chunk // 2
    dist = nz // 2
    me = lax.axis_index("seq")
    z = lax.axis_index("tp")
    q, core = me // 2, lax.rem(me, 2)
    other = q * 2 + (1 - core)
    up, down = lax.rem(z + 1, nz), lax.rem(z + nz - 1, nz)
    seq_count = nq * 2

    def remote(src, dst, send, recv, seq_id, z_id):
        return pltpu.make_async_remote_copy(
            src_ref=src, dst_ref=dst, send_sem=send, recv_sem=recv,
            device_id=(seq_id, z_id), device_id_type=MESH,
        )

    def xy_peer(o):
        peer = lax.rem(q + o, nq)
        return peer, peer * 2 + core

    def seq_peer(o):
        return lax.rem(me + o, seq_count)

    def chunk_of(j):
        return lax.rem(z + j, nz)

    sk_copies = [
        pltpu.make_async_copy(sk_hbm.at[:, pl.ds(h * HALF, HALF)], sk.at[h], sk_sem.at[h])
        for h in range(2)
    ]
    tok_copies = {}
    order = [dist]
    for s in range(1, dist):
        order += [dist - s, nz - dist + s]
    order.append(0)
    for j in order:
        at = pl.ds(pl.multiple_of(chunk_of(j) * chunk, chunk), chunk)
        tok_copies[j] = pltpu.make_async_copy(tok_hbm.at[at], tok.at[at], tok_sem.at[j])
    sk_copies[0].start()
    tok_copies[order[0]].start()
    sk_copies[1].start()
    for j in order[1:]:
        tok_copies[j].start()

    barrier = pltpu.get_barrier_semaphore()

    def greet_seq(o, carry):
        pl.semaphore_signal(barrier, inc=1, device_id=(seq_peer(o), z), device_id_type=MESH)
        return carry

    def greet_z(o, carry):
        pl.semaphore_signal(
            barrier, inc=1, device_id=(me, lax.rem(z + o, nz)), device_id_type=MESH
        )
        return carry

    lax.fori_loop(1, nz, greet_z, 0)
    lax.fori_loop(1, seq_count, greet_seq, 0)

    loaded = set()

    def prepare_weights(h):
        sk_copies[h].wait()
        step = min(256, feats)

        @pl.loop(0, feats // step)
        def _(i):
            at = pl.ds(pl.multiple_of(i * step, step), step)
            high, low = split_parts(sk[h, at, :])
            weights[h, at, :HALF] = high
            weights[h, at, HALF:] = low

    def compute_part(h, j):
        if j not in loaded:
            tok_copies[j].wait()
            loaded.add(j)
        at = pl.ds(pl.multiple_of(chunk_of(j) * chunk, chunk), chunk)
        both = jnp.dot(tok[at, :], weights[h], preferred_element_type=F32)
        part[h, j] = both[:, :HALF] + both[:, HALF:]

    def unit_rows(u):
        return pl.ds(u * unit, unit)

    sent = []

    def rs_copy(h, d, s, u, src):
        slot = s * 2 + u
        return remote(
            src, ring.at[h, d, slot], rs_send.at[h, d, slot], rs_recv.at[h, d, slot],
            me, up if d == 0 else down,
        )

    def rs_send_unit(h, d, s, u, src):
        copy = rs_copy(h, d, s, u, src)
        copy.start()
        sent.append(copy)

    def rs_wait(h, d, s, u):
        rs_copy(h, d, s, u, ring.at[h, d, s * 2 + u]).wait_recv()

    def own_chunk(h):
        at = pl.multiple_of(z * chunk, chunk)
        for u in range(2):
            for d in range(2):
                rs_wait(h, d, dist - 1, u)
        for u in range(2):
            slot = (dist - 1) * 2 + u
            value = part[h, 0, unit_rows(u), :] + ring[h, 0, slot] + ring[h, 1, slot]
            s_all[h, pl.ds(at + u * unit, unit), :] = value

    def ag_copy(h, d, k, u):
        c = lax.rem(z + nz - k, nz) if d == 0 else lax.rem(z + k, nz)
        at = pl.ds(pl.multiple_of(c * chunk + u * unit, unit), unit)
        slot = k * 2 + u
        return remote(
            s_all.at[h, at], s_all.at[h, at], ag_send.at[h, d, slot], ag_recv.at[h, d, slot],
            me, up if d == 0 else down,
        )

    def ag_arrived(h, d, k, u):
        c = lax.rem(z + nz - k - 1, nz) if d == 0 else lax.rem(z + k + 1, nz)
        at = pl.ds(pl.multiple_of(c * chunk + u * unit, unit), unit)
        slot = k * 2 + u
        remote(
            s_all.at[h, at], s_all.at[h, at], ag_send.at[h, d, slot], ag_recv.at[h, d, slot],
            me, up if d == 0 else down,
        ).wait_recv()

    if dist == 4:
        turns = [
            (0, 0, 1, 0), (0, 0, 0, 1), (0, 1, 1, 0), (0, 0, 1, 1), (0, 0, 0, 2), (0, 1, 1, 1),
            (0, 0, 1, 2), (0, 0, 0, 3), (0, 1, 0, 1), (0, 0, 1, 3), (0, 1, 1, 2), (0, 1, 0, 2),
            (1, 0, 1, 0), (0, 1, 1, 3), (0, 1, 0, 3), (1, 0, 0, 0), (1, 0, 1, 1), (1, 1, 1, 0),
            (1, 0, 0, 1), (1, 0, 1, 2), (1, 1, 0, 0), (1, 0, 0, 2), (1, 0, 1, 3), (1, 1, 1, 1),
            (1, 1, 0, 1), (1, 1, 1, 2), (1, 1, 0, 2), (1, 1, 1, 3),
        ]
    else:
        turns = [(0, h, x, k) for k in range(dist) for h in range(2) for x in (1, 0) if k or x]
        turns += [
            (1, h, x, k) for k in range(dist) for h in range(2) for x in (1, 0) if k < dist - 1 or x
        ]

    def places(k):
        return dist - k, (nz - dist + k) % nz

    have = set()

    def ensure(h, j):
        if (h, j) not in have:
            if not any(half == h for half, _ in have):
                prepare_weights(h)
            compute_part(h, j)
            have.add((h, j))

    def ring_turn(i):
        gather, h, long, k = turns[i]
        for d in range(2):
            u = d if long else 1 - d
            if gather:
                if k > 0:
                    ag_arrived(h, d, k - 1, u)
                copy = ag_copy(h, d, k, u)
                copy.start()
                sent.append(copy)
                continue
            j = places(k)[d]
            ensure(h, j)
            if i == 0 and d == 0:
                pl.semaphore_wait(barrier, seq_count - 1 + nz - 1)
            if k == (0 if long else 1):
                rs_send_unit(h, d, k, u, part.at[h, j, unit_rows(u)])
            else:
                rs_wait(h, d, k - 1, u)
                slot = (k - 1) * 2 + u
                ring[h, d, slot] = ring[h, d, slot] + part[h, j, unit_rows(u), :]
                rs_send_unit(h, d, k, u, ring.at[h, d, slot])
        for ahead in turns[i + 1 : i + 3]:
            if not ahead[0]:
                for j in places(ahead[3]):
                    ensure(ahead[1], j)

    progress = []

    def ring_to(count):
        while len(progress) < count:
            ring_turn(len(progress))
            progress.append(1)

    def gather_last(h, long):
        for d in range(2):
            if long:
                ag_arrived(h, d, dist - 1, d)
            else:
                ag_arrived(h, d, dist - 2, 1 - d)

    def probe_of(sized, step):
        return remote(sized, sized, g_send.at[step], g_recv.at[step], me, up)

    def gram_sum():
        piece = gsrc.shape[0] // seq_count

        def rows_of(i):
            return pl.ds(pl.multiple_of(i * piece, piece), piece)

        def first(o, carry):
            peer = seq_peer(o)
            remote(
                gsrc.at[rows_of(peer)], ga.at[me], g_send.at[0], g_recv.at[0], peer, z
            ).start()
            return carry

        lax.fori_loop(1, seq_count, first, 0)
        ga[me] = gsrc[rows_of(me), :]
        yield
        probe = probe_of(ga.at[pl.ds(0, seq_count - 1)], 0)
        probe.wait_recv()
        value = ga[0]
        for i in range(1, seq_count):
            value = value + ga[i]
        gb[z] = value

        def second(o, carry):
            remote(
                gb.at[z], gb.at[z], g_send.at[1], g_recv.at[1], me, lax.rem(z + o, nz)
            ).start()
            return carry

        lax.fori_loop(1, nz, second, 0)
        probe.wait_send()
        yield
        probe = probe_of(gb.at[pl.ds(0, nz - 1)], 1)
        probe.wait_recv()
        value = gb[0]
        for i in range(1, nz):
            value = value + gb[i]
        gfull[rows_of(me), :] = value

        def third(o, carry):
            remote(
                gfull.at[rows_of(me)], gfull.at[rows_of(me)], g_send.at[2], g_recv.at[2],
                seq_peer(o), z,
            ).start()
            return carry

        lax.fori_loop(1, seq_count, third, 0)
        probe.wait_send()
        yield
        probe = probe_of(gfull.at[pl.ds(0, (seq_count - 1) * piece)], 2)
        probe.wait_recv()
        probe.wait_send()
        yield

    tile = min(512, feats)
    per_tile = tile // HALF

    def product(h, j, first, after_tile=None):
        at = pl.ds(pl.multiple_of(chunk_of(j) * chunk, chunk), chunk)
        high, low = split_parts(s_all[h, at, :].T)
        left = jnp.concatenate([high, low], axis=0)
        for t in range(feats // tile):
            both = jnp.dot(left, tok[at, t * tile : (t + 1) * tile], preferred_element_type=F32)
            value = both[:HALF] + both[HALF:]
            for i in range(per_tile):
                item = value[:, i * HALF : (i + 1) * HALF]
                p = t * per_tile + i
                c0[h, p] = item if first else c0[h, p] + item
            if after_tile is not None:
                after_tile(t)

    split = HALF // 2

    def core_copy(h, t):
        give = pl.ds(pl.multiple_of((1 - core) * split, split), split)
        at = pl.ds(t * per_tile, per_tile)
        return remote(
            c0.at[h, at, give], cx.at[h, at], c_send.at[h, t], c_recv.at[h, t], other, z
        )

    tiles = feats // tile

    def start_core(h):
        def after(t):
            copy = core_copy(h, t)
            copy.start()
            sent.append(copy)

        return after

    def coef_sum(h):
        keep = pl.ds(pl.multiple_of(core * split, split), split)
        for t in range(tiles):
            core_copy(h, t).wait_recv()
            for i in range(per_tile):
                p = t * per_tile + i
                cp[h, p] = c0[h, p, keep, :] + cx[h, p]

        def body(o, carry):
            peer, seq_id = xy_peer(o)
            remote(
                cp.at[h, peer], cr.at[h, q], c_send.at[h, tiles], c_recv.at[h, tiles], seq_id, z
            ).start()
            return carry

        lax.fori_loop(1, nq, body, 0)
        cr[h, q] = cp[h, q]
        yield
        sized = cr.at[h, pl.ds(0, nq - 1)]
        probe = remote(sized, sized, c_send.at[h, tiles], c_recv.at[h, tiles], me, up)
        probe.wait_recv()
        probe.wait_send()
        value = cr[h, 0]
        for i in range(1, nq):
            value = value + cr[h, i]
        cg[h, keep, :] = value
        copy = remote(
            cg.at[h, keep], cg.at[h, keep], c_send.at[h, tiles + 1], c_recv.at[h, tiles + 1],
            other, z,
        )
        copy.start()
        yield
        copy.wait()
        yield

    def run(gen, steps=None):
        count = 0
        while steps is None or count < steps:
            try:
                next(gen)
            except StopIteration as stop:
                return stop.value
            count += 1
        return None

    coef = [coef_sum(h) for h in range(2)]
    own = pl.ds(pl.multiple_of(z * chunk, chunk), chunk)
    def pair(h, k):
        product(h, nz - k, False)
        product(h, k, False)

    full = dist == 4
    ring_to(12 if full else len(turns) // 2)
    ensure(0, 0)
    own_chunk(0)
    ring_to(15 if full else 0)
    own0 = s_all[0, own, :]
    gsrc[:HALF] = tn(own0, own0)
    gsrc[3 * HALF :] = jnp.zeros((HALF, HALF), F32)
    ensure(1, 0)
    ring_to(17 if full else 0)
    own_chunk(1)
    ring_to(18 if full else 0)
    own1 = s_all[1, own, :]
    gsrc[HALF : 2 * HALF] = tn(own1, s_all[0, own, :])
    gsrc[2 * HALF : 3 * HALF] = tn(own1, own1)
    gram = gram_sum()
    run(gram, 1)
    ring_to(19 if full else 0)
    product(0, 0, True)
    product(1, 0, True)
    if full:
        ring_to(20)
        pair(0, 1)
        ring_to(23)
        run(gram, 1)
        pair(0, 2)
        ring_to(24)
        gather_last(0, 0)
        pair(0, 3)
        ring_to(25)
        gather_last(0, 1)
        product(0, 4, False, start_core(0))
        ring_to(26)
        run(gram, 1)
        run(coef[0], 1)
        pair(1, 1)
        ring_to(27)
        pair(1, 2)
        ring_to(28)
        gather_last(1, 0)
        pair(1, 3)
        gather_last(1, 1)
        product(1, 4, False, start_core(1))
    else:
        ring_to(len(turns))
        run(gram, 2)
        for h in range(2):
            gather_last(h, 0)
            gather_last(h, 1)
            for j in order[:-1]:
                product(h, j, False, start_core(h) if j == order[-2] else None)
        run(coef[0], 1)
    run(gram, 1)
    chol0 = inverse_factor(gfull[:HALF])
    run(chol0, 3)
    run(coef[1], 1)
    w00 = run(chol0)
    run(coef[0], 1)
    low10 = nt(gfull[HALF : 2 * HALF], w00)
    chol1 = inverse_factor(gfull[2 * HALF : 3 * HALF] - nt(low10, low10))
    mixed = nn(low10, w00)
    w11 = run(chol1)
    w10 = -nn(w11, mixed)
    root = math.sqrt(total)
    step = min(256, rows)

    def basis_half(h):
        @pl.loop(0, rows // step)
        def _(i):
            at = pl.ds(pl.multiple_of(i * step, step), step)
            if h == 0:
                basis_out[at, :HALF] = nt(s_all[0, at, :], w00 * root)
            else:
                basis_out[at, HALF:] = nt(s_all[0, at, :], w10 * root) + nt(
                    s_all[1, at, :], w11 * root
                )

    basis_half(0)
    run(coef[0])
    run(coef[1])
    block = 2 * HALF // seq_count
    outs[:HALF] = nn(w00, cg[0]) / root
    outs[HALF:] = (nn(w10, cg[0]) + nn(w11, cg[1])) / root

    def rows_for(seq_id):
        return pl.ds(pl.multiple_of(seq_id * block, block), block)

    def last_hop(o, carry):
        _, seq_id = xy_peer(o)
        remote(
            outs.at[rows_for(seq_id)], landed.at[q], c_send.at[2, 0], c_recv.at[2, 0], seq_id, z
        ).start()
        return carry

    lax.fori_loop(1, nq, last_hop, 0)
    landed[q] = outs[rows_for(me), :]

    basis_half(1)
    sized = landed.at[pl.ds(0, nq - 1)]
    probe = remote(sized, sized, c_send.at[2, 0], c_recv.at[2, 0], me, up)
    probe.wait_recv()
    probe.wait_send()
    for i in range(nq):
        coef_out[:, i * HALF : (i + 1) * HALF] = landed[i]

    for copy in sent:
        copy.wait_send()


def shards(mesh_shape, tokens, sketch):
    rows, feats = tokens.shape
    seq, nz = mesh_shape["seq"], mesh_shape["tp"]
    nq = seq // 2
    total = rows * seq
    chunk = rows // nz
    unit = chunk // 2
    dist = nz // 2
    k = 2 * HALF
    dma = pltpu.SemaphoreType.DMA
    tiles = feats // min(512, feats)
    return pl.pallas_call(
        functools.partial(kernel, nq, nz, total),
        out_shape=(
            jax.ShapeDtypeStruct((rows, k), F32),
            jax.ShapeDtypeStruct((k // seq, feats), F32),
        ),
        in_specs=[pl.BlockSpec(memory_space=pl.ANY)] * 2,
        out_specs=(pl.BlockSpec(memory_space=pltpu.VMEM),) * 2,
        scratch_shapes=[
            pltpu.VMEM((rows, feats), BF16),
            pltpu.VMEM((2, feats, HALF), F32),
            pltpu.VMEM((2, feats, k), BF16),
            pltpu.VMEM((2, nz, chunk, HALF), F32),
            pltpu.VMEM((2, 2, nz, unit, HALF), F32),
            pltpu.VMEM((2, rows, HALF), F32),
            pltpu.VMEM((4 * HALF, HALF), F32),
            pltpu.VMEM((seq, 4 * HALF // seq, HALF), F32),
            pltpu.VMEM((nz, 4 * HALF // seq, HALF), F32),
            pltpu.VMEM((4 * HALF, HALF), F32),
            pltpu.VMEM((2, nq, HALF, HALF), F32),
            pltpu.VMEM((2, nq, HALF // 2, HALF), F32),
            pltpu.VMEM((2, nq, HALF // 2, HALF), F32),
            pltpu.VMEM((2, nq, HALF // 2, HALF), F32),
            pltpu.VMEM((2, HALF, HALF), F32),
            pltpu.VMEM((k, HALF), F32),
            pltpu.VMEM((nq, k // seq, HALF), F32),
            dma((nz,)),
            dma((2,)),
            dma((2, 2, nz)),
            dma((2, 2, nz)),
            dma((2, 2, nz)),
            dma((2, 2, nz)),
            dma((3,)),
            dma((3,)),
            dma((3, tiles + 2)),
            dma((3, tiles + 2)),
        ],
        compiler_params=pltpu.CompilerParams(
            collective_id=0, has_side_effects=True, vmem_limit_bytes=50 * 1024 * 1024
        ),
    )(tokens, sketch)


def solution(mesh):
    return jax.shard_map(
        functools.partial(shards, dict(mesh.shape)),
        mesh=mesh,
        in_specs=(P("seq", "tp"), P("tp", None)),
        out_specs=(P("seq", None), P("seq", "tp")),
        check_vma=False,
    )
```

```python
import functools
import math

import jax
import jax.numpy as jnp
from jax import lax
from jax.experimental import pallas as pl
from jax.experimental.pallas import tpu as pltpu
from jax.sharding import PartitionSpec as P

MESH = pl.DeviceIdType.MESH
HIGHEST = lax.Precision.HIGHEST
F32 = jnp.float32
BF16 = jnp.bfloat16
HALF = 128
PANEL = 16
SUBS = 1


def dot32(a, b, dims):
    return lax.dot_general(a, b, (dims, ((), ())), precision=HIGHEST, preferred_element_type=F32)


def nn(a, b):
    return dot32(a, b, ((1,), (0,)))


def nt(a, b):
    return dot32(a, b, ((1,), (1,)))


def tn(a, b):
    return dot32(a, b, ((0,), (0,)))


def split_parts(value):
    high = value.astype(BF16)
    low = (value - high.astype(F32)).astype(BF16)
    return high, low


def inverse_factor(matrix):
    size = matrix.shape[0]
    sub = lax.broadcasted_iota(jnp.int32, (PANEL, HALF), 0)
    lane = lax.broadcasted_iota(jnp.int32, (PANEL, HALF), 1)
    rest = matrix
    done = []
    for first in range(0, size, PANEL):
        panel = rest[:PANEL]
        below = rest[PANEL:]
        columns = [
            jnp.broadcast_to(panel[:, first + j : first + j + 1], (PANEL, HALF)) for j in range(PANEL)
        ]
        inside = (lane >= first) & (lane < first + PANEL)
        panel = jnp.where(inside, jnp.where(lane - first == sub, 1.0, 0.0), panel)
        work = columns + [panel]
        kept = jnp.zeros((PANEL, HALF), F32)
        pivots = jnp.ones((PANEL, HALF), F32)
        for j in range(PANEL):
            here = sub == j
            rows = [jnp.broadcast_to(item[j : j + 1], (PANEL, HALF)) for item in work]
            pivot = rows[0]
            inverse = 1.0 / work[0]
            scale = jnp.broadcast_to(inverse[j : j + 1], (PANEL, HALF))
            factor = jnp.where(here, -1.0, work[0]) * scale
            kept = jnp.where(here, rows[-1], kept)
            pivots = jnp.where(here, pivot, pivots)
            work = [
                jnp.where(here, 0.0, item) - factor * row for item, row in zip(work[1:], rows[1:])
            ]
        scaled = kept * lax.rsqrt(pivots)
        done.append(jnp.where(lane <= sub + first, scaled, 0.0))
        if first + PANEL < size:
            solved = work[0]
            count = size - first - PANEL
            pieces = []
            for begin, end in ((0, PANEL), (PANEL, count)):
                if begin >= end:
                    continue
                low = below[begin:end]
                low_lane = lax.broadcasted_iota(jnp.int32, (end - begin, HALF), 1)
                update = jnp.where((low_lane >= first) & (low_lane < first + PANEL), 0.0, low)
                terms = [low[:, first + j : first + j + 1] * solved[j : j + 1] for j in range(PANEL)]
                while len(terms) > 1:
                    terms = [a + b for a, b in zip(terms[::2], terms[1::2])]
                pieces.append(update - terms[0])
            rest = jnp.concatenate(pieces, axis=0) if len(pieces) > 1 else pieces[0]
        yield None
    return jnp.concatenate(done, axis=0)


def kernel(
    nq, nz, total,
    tok_hbm, sk_hbm, basis_out, coef_out,
    tok, sk, weights, part, ring, s_all,
    gsrc, ga, gb, gfull,
    c0, cx, cp, cr, cg, outs, landed,
    tok_sem, sk_sem, rs_send, rs_recv, ag_send, ag_recv, g_send, g_recv,
    c_send, c_recv,
):
    rows, feats = tok.shape
    chunk = rows // nz
    unit = chunk // 2
    piece_rows = unit // SUBS
    dist = nz // 2
    me = lax.axis_index("seq")
    z = lax.axis_index("tp")
    q, core = me // 2, lax.rem(me, 2)
    other = q * 2 + (1 - core)
    up, down = lax.rem(z + 1, nz), lax.rem(z + nz - 1, nz)
    seq_count = nq * 2

    def remote(src, dst, send, recv, seq_id, z_id):
        return pltpu.make_async_remote_copy(
            src_ref=src, dst_ref=dst, send_sem=send, recv_sem=recv,
            device_id=(seq_id, z_id), device_id_type=MESH,
        )

    def xy_peer(o):
        peer = lax.rem(q + o, nq)
        return peer, peer * 2 + core

    def seq_peer(o):
        return lax.rem(me + o, seq_count)

    def chunk_of(j):
        return lax.rem(z + j, nz)

    sk_copies = [
        pltpu.make_async_copy(sk_hbm.at[:, pl.ds(h * HALF, HALF)], sk.at[h], sk_sem.at[h])
        for h in range(2)
    ]
    tok_copies = {}
    order = [dist]
    for s in range(1, dist):
        order += [dist - s, nz - dist + s]
    order.append(0)
    for j in order:
        at = pl.ds(pl.multiple_of(chunk_of(j) * chunk, chunk), chunk)
        tok_copies[j] = pltpu.make_async_copy(tok_hbm.at[at], tok.at[at], tok_sem.at[j])
    sk_copies[0].start()
    tok_copies[order[0]].start()
    sk_copies[1].start()
    for j in order[1:]:
        tok_copies[j].start()

    barrier = pltpu.get_barrier_semaphore()

    def greet_seq(o, carry):
        pl.semaphore_signal(barrier, inc=1, device_id=(seq_peer(o), z), device_id_type=MESH)
        return carry

    def greet_z(o, carry):
        pl.semaphore_signal(
            barrier, inc=1, device_id=(me, lax.rem(z + o, nz)), device_id_type=MESH
        )
        return carry

    lax.fori_loop(1, nz, greet_z, 0)
    lax.fori_loop(1, seq_count, greet_seq, 0)

    loaded = set()

    def prepare_weights(h):
        sk_copies[h].wait()
        step = min(256, feats)

        @pl.loop(0, feats // step)
        def _(i):
            at = pl.ds(pl.multiple_of(i * step, step), step)
            high, low = split_parts(sk[h, at, :])
            weights[h, at, :HALF] = high
            weights[h, at, HALF:] = low

    def compute_part(h, j):
        if j not in loaded:
            tok_copies[j].wait()
            loaded.add(j)
        at = pl.ds(pl.multiple_of(chunk_of(j) * chunk, chunk), chunk)
        both = jnp.dot(tok[at, :], weights[h], preferred_element_type=F32)
        part[h, j] = both[:, :HALF] + both[:, HALF:]

    def part_rows(u, b):
        return pl.ds(u * unit + b * piece_rows, piece_rows)

    sent = []

    def rs_copy(h, d, s, u, b, src):
        slot = s * 2 + u
        return remote(
            src, ring.at[h, d, slot, b], rs_send.at[h, d, slot, b], rs_recv.at[h, d, slot, b],
            me, up if d == 0 else down,
        )

    def rs_send_unit(h, d, s, u, b, src):
        copy = rs_copy(h, d, s, u, b, src)
        copy.start()
        sent.append(copy)

    def rs_wait(h, d, s, u, b):
        rs_copy(h, d, s, u, b, ring.at[h, d, s * 2 + u, b]).wait_recv()

    def own_chunk(h):
        at = pl.multiple_of(z * chunk, chunk)
        slot = (dist - 1) * 2
        for u in range(2):
            for b in range(SUBS):
                for d in range(2):
                    rs_wait(h, d, dist - 1, u, b)
                value = part[h, 0, part_rows(u, b), :]
                value = value + ring[h, 0, slot + u, b] + ring[h, 1, slot + u, b]
                s_all[h, pl.ds(at + u * unit + b * piece_rows, piece_rows), :] = value

    def ag_unit(h, d, k, u, b, c):
        start = c * chunk + u * unit + b * piece_rows
        at = pl.ds(pl.multiple_of(start, piece_rows), piece_rows)
        slot = k * 2 + u
        return remote(
            s_all.at[h, at], s_all.at[h, at], ag_send.at[h, d, slot, b], ag_recv.at[h, d, slot, b],
            me, up if d == 0 else down,
        )

    def ag_copy(h, d, k, u, b):
        c = lax.rem(z + nz - k, nz) if d == 0 else lax.rem(z + k, nz)
        return ag_unit(h, d, k, u, b, c)

    def ag_arrived(h, d, k, u, b):
        c = lax.rem(z + nz - k - 1, nz) if d == 0 else lax.rem(z + k + 1, nz)
        ag_unit(h, d, k, u, b, c).wait_recv()

    if dist == 4:
        turns = [
            (0, 0, 1, 0), (0, 0, 0, 1), (0, 1, 1, 0), (0, 0, 1, 1), (0, 0, 0, 2), (0, 1, 1, 1),
            (0, 0, 1, 2), (0, 0, 0, 3), (0, 1, 0, 1), (0, 0, 1, 3), (0, 1, 1, 2), (0, 1, 0, 2),
            (1, 0, 1, 0), (0, 1, 1, 3), (0, 1, 0, 3), (1, 0, 0, 0), (1, 0, 1, 1), (1, 1, 1, 0),
            (1, 0, 0, 1), (1, 0, 1, 2), (1, 1, 0, 0), (1, 0, 0, 2), (1, 0, 1, 3), (1, 1, 1, 1),
            (1, 1, 0, 1), (1, 1, 1, 2), (1, 1, 0, 2), (1, 1, 1, 3),
        ]
    else:
        turns = [(0, h, x, k) for k in range(dist) for h in range(2) for x in (1, 0) if k or x]
        turns += [
            (1, h, x, k) for k in range(dist) for h in range(2) for x in (1, 0) if k < dist - 1 or x
        ]

    def places(k):
        return dist - k, (nz - dist + k) % nz

    have = set()

    def ensure(h, j):
        if (h, j) not in have:
            if not any(half == h for half, _ in have):
                prepare_weights(h)
            compute_part(h, j)
            have.add((h, j))

    def ring_turn(i):
        gather, h, long, k = turns[i]
        if not gather:
            for j in places(k):
                ensure(h, j)
            if i == 0:
                pl.semaphore_wait(barrier, seq_count - 1 + nz - 1)
        for b in range(SUBS):
            for d in range(2):
                u = d if long else 1 - d
                if gather:
                    if k > 0:
                        ag_arrived(h, d, k - 1, u, b)
                    copy = ag_copy(h, d, k, u, b)
                    copy.start()
                    sent.append(copy)
                    continue
                j = places(k)[d]
                if k == (0 if long else 1):
                    rs_send_unit(h, d, k, u, b, part.at[h, j, part_rows(u, b)])
                else:
                    rs_wait(h, d, k - 1, u, b)
                    slot = (k - 1) * 2 + u
                    ring[h, d, slot, b] = ring[h, d, slot, b] + part[h, j, part_rows(u, b), :]
                    rs_send_unit(h, d, k, u, b, ring.at[h, d, slot, b])
        for ahead in turns[i + 1 : i + 3]:
            if not ahead[0]:
                for j in places(ahead[3]):
                    ensure(ahead[1], j)

    progress = []

    def ring_to(count):
        while len(progress) < count:
            ring_turn(len(progress))
            progress.append(1)

    def gather_last(h, long):
        for b in range(SUBS):
            for d in range(2):
                if long:
                    ag_arrived(h, d, dist - 1, d, b)
                else:
                    ag_arrived(h, d, dist - 2, 1 - d, b)

    def probe_of(sized, step):
        return remote(sized, sized, g_send.at[step], g_recv.at[step], me, up)

    def gram_sum():
        piece = gsrc.shape[0] // seq_count

        def rows_of(i):
            return pl.ds(pl.multiple_of(i * piece, piece), piece)

        def first(o, carry):
            peer = seq_peer(o)
            remote(
                gsrc.at[rows_of(peer)], ga.at[me], g_send.at[0], g_recv.at[0], peer, z
            ).start()
            return carry

        lax.fori_loop(1, seq_count, first, 0)
        ga[me] = gsrc[rows_of(me), :]
        yield
        probe = probe_of(ga.at[pl.ds(0, seq_count - 1)], 0)
        probe.wait_recv()
        value = ga[0]
        for i in range(1, seq_count):
            value = value + ga[i]
        gb[z] = value

        def second(o, carry):
            remote(
                gb.at[z], gb.at[z], g_send.at[1], g_recv.at[1], me, lax.rem(z + o, nz)
            ).start()
            return carry

        lax.fori_loop(1, nz, second, 0)
        probe.wait_send()
        yield
        probe = probe_of(gb.at[pl.ds(0, nz - 1)], 1)
        probe.wait_recv()
        value = gb[0]
        for i in range(1, nz):
            value = value + gb[i]
        gfull[rows_of(me), :] = value

        def third(o, carry):
            remote(
                gfull.at[rows_of(me)], gfull.at[rows_of(me)], g_send.at[2], g_recv.at[2],
                seq_peer(o), z,
            ).start()
            return carry

        lax.fori_loop(1, seq_count, third, 0)
        probe.wait_send()
        yield
        probe = probe_of(gfull.at[pl.ds(0, (seq_count - 1) * piece)], 2)
        probe.wait_recv()
        probe.wait_send()
        yield

    tile = min(512, feats)
    per_tile = tile // HALF

    def product(h, j, first, after_tile=None):
        at = pl.ds(pl.multiple_of(chunk_of(j) * chunk, chunk), chunk)
        high, low = split_parts(s_all[h, at, :].T)
        left = jnp.concatenate([high, low], axis=0)
        for t in range(feats // tile):
            both = jnp.dot(left, tok[at, t * tile : (t + 1) * tile], preferred_element_type=F32)
            value = both[:HALF] + both[HALF:]
            for i in range(per_tile):
                item = value[:, i * HALF : (i + 1) * HALF]
                p = t * per_tile + i
                c0[h, p] = item if first else c0[h, p] + item
            if after_tile is not None:
                after_tile(t)

    split = HALF // 2

    def core_copy(h, t):
        give = pl.ds(pl.multiple_of((1 - core) * split, split), split)
        at = pl.ds(t * per_tile, per_tile)
        return remote(
            c0.at[h, at, give], cx.at[h, at], c_send.at[h, t], c_recv.at[h, t], other, z
        )

    tiles = feats // tile

    def start_core(h):
        def after(t):
            copy = core_copy(h, t)
            copy.start()
            sent.append(copy)

        return after

    def coef_sum(h):
        keep = pl.ds(pl.multiple_of(core * split, split), split)
        for t in range(tiles):
            core_copy(h, t).wait_recv()
            for i in range(per_tile):
                p = t * per_tile + i
                cp[h, p] = c0[h, p, keep, :] + cx[h, p]

                @pl.when(p != q)
                def _(p=p):
                    remote(
                        cp.at[h, p], cr.at[h, q], c_send.at[h, tiles], c_recv.at[h, tiles],
                        p * 2 + core, z,
                    ).start()

        cr[h, q] = cp[h, q]
        yield
        sized = cr.at[h, pl.ds(0, nq - 1)]
        probe = remote(sized, sized, c_send.at[h, tiles], c_recv.at[h, tiles], me, up)
        probe.wait_recv()
        probe.wait_send()
        value = cr[h, 0]
        for i in range(1, nq):
            value = value + cr[h, i]
        cg[h, keep, :] = value
        copy = remote(
            cg.at[h, keep], cg.at[h, keep], c_send.at[h, tiles + 1], c_recv.at[h, tiles + 1],
            other, z,
        )
        copy.start()
        yield
        copy.wait()
        yield

    def run(gen, steps=None):
        count = 0
        while steps is None or count < steps:
            try:
                next(gen)
            except StopIteration as stop:
                return stop.value
            count += 1
        return None

    coef = [coef_sum(h) for h in range(2)]
    own = pl.ds(pl.multiple_of(z * chunk, chunk), chunk)
    def pair(h, k):
        product(h, nz - k, False)
        product(h, k, False)

    full = dist == 4
    ring_to(12 if full else len(turns) // 2)
    ensure(0, 0)
    own_chunk(0)
    ring_to(15 if full else 0)
    own0 = s_all[0, own, :]
    gsrc[:HALF] = tn(own0, own0)
    gsrc[3 * HALF :] = jnp.zeros((HALF, HALF), F32)
    ensure(1, 0)
    ring_to(17 if full else 0)
    own_chunk(1)
    ring_to(18 if full else 0)
    own1 = s_all[1, own, :]
    gsrc[HALF : 2 * HALF] = tn(own1, s_all[0, own, :])
    gsrc[2 * HALF : 3 * HALF] = tn(own1, own1)
    gram = gram_sum()
    run(gram, 1)
    ring_to(19 if full else 0)
    product(0, 0, True)
    product(1, 0, True)
    if full:
        ring_to(20)
        pair(0, 1)
        ring_to(22)
        run(gram, 1)
        ring_to(23)
        pair(0, 2)
        ring_to(24)
        gather_last(0, 0)
        pair(0, 3)
        ring_to(25)
        gather_last(0, 1)
        product(0, 4, False, start_core(0))
        ring_to(26)
        run(gram, 1)
        run(coef[0], 1)
        pair(1, 1)
        ring_to(27)
        pair(1, 2)
        ring_to(28)
        gather_last(1, 0)
        pair(1, 3)
        gather_last(1, 1)
        product(1, 4, False, start_core(1))
    else:
        ring_to(len(turns))
        run(gram, 2)
        for h in range(2):
            gather_last(h, 0)
            gather_last(h, 1)
            for j in order[:-1]:
                product(h, j, False, start_core(h) if j == order[-2] else None)
        run(coef[0], 1)
    run(coef[1], 1)
    run(gram, 1)
    chol0 = inverse_factor(gfull[:HALF])
    run(chol0, 4)
    run(coef[0], 1)
    w00 = run(chol0)
    low10 = nt(gfull[HALF : 2 * HALF], w00)
    chol1 = inverse_factor(gfull[2 * HALF : 3 * HALF] - nt(low10, low10))
    mixed = nn(low10, w00)
    w11 = run(chol1)
    w10 = -nn(w11, mixed)
    root = math.sqrt(total)
    step = min(256, rows)

    def make_basis():
        upper = jnp.concatenate([w00, jnp.zeros((HALF, HALF), F32)], axis=1)
        factor = jnp.concatenate([upper, jnp.concatenate([w10, w11], axis=1)], axis=0) * root

        @pl.loop(0, rows // step)
        def _(i):
            at = pl.ds(pl.multiple_of(i * step, step), step)
            left = jnp.concatenate([s_all[0, at, :], s_all[1, at, :]], axis=1)
            basis_out[at, :] = nt(left, factor)

    block = 2 * HALF // seq_count

    def rows_for(seq_id):
        return pl.ds(pl.multiple_of(seq_id * block, block), block)

    def deliver(first, count):
        def body(p, carry):
            @pl.when(p != q)
            def _():
                seq_id = p * 2 + core
                remote(
                    outs.at[rows_for(seq_id)], landed.at[q], c_send.at[2, 0], c_recv.at[2, 0],
                    seq_id, z,
                ).start()

            return carry

        lax.fori_loop(first, first + count, body, 0)

    run(coef[0])
    reduced0 = cg[0]
    outs[:HALF] = nn(w00, reduced0) / root
    deliver(0, nq // 2)
    early = nn(w10, reduced0)
    run(coef[1])
    outs[HALF:] = (early + nn(w11, cg[1])) / root
    deliver(nq // 2, nq // 2)
    landed[q] = outs[rows_for(me), :]
    for copy in sent:
        copy.wait_send()

    make_basis()
    sized = landed.at[pl.ds(0, nq - 1)]
    probe = remote(sized, sized, c_send.at[2, 0], c_recv.at[2, 0], me, up)
    probe.wait_recv()
    probe.wait_send()
    for i in range(nq):
        coef_out[:, i * HALF : (i + 1) * HALF] = landed[i]


def shards(mesh_shape, tokens, sketch):
    rows, feats = tokens.shape
    seq, nz = mesh_shape["seq"], mesh_shape["tp"]
    nq = seq // 2
    total = rows * seq
    chunk = rows // nz
    unit = chunk // 2
    dist = nz // 2
    k = 2 * HALF
    dma = pltpu.SemaphoreType.DMA
    tiles = feats // min(512, feats)
    return pl.pallas_call(
        functools.partial(kernel, nq, nz, total),
        out_shape=(
            jax.ShapeDtypeStruct((rows, k), F32),
            jax.ShapeDtypeStruct((k // seq, feats), F32),
        ),
        in_specs=[pl.BlockSpec(memory_space=pl.ANY)] * 2,
        out_specs=(pl.BlockSpec(memory_space=pltpu.VMEM),) * 2,
        scratch_shapes=[
            pltpu.VMEM((rows, feats), BF16),
            pltpu.VMEM((2, feats, HALF), F32),
            pltpu.VMEM((2, feats, k), BF16),
            pltpu.VMEM((2, nz, chunk, HALF), F32),
            pltpu.VMEM((2, 2, nz, SUBS, unit // SUBS, HALF), F32),
            pltpu.VMEM((2, rows, HALF), F32),
            pltpu.VMEM((4 * HALF, HALF), F32),
            pltpu.VMEM((seq, 4 * HALF // seq, HALF), F32),
            pltpu.VMEM((nz, 4 * HALF // seq, HALF), F32),
            pltpu.VMEM((4 * HALF, HALF), F32),
            pltpu.VMEM((2, nq, HALF, HALF), F32),
            pltpu.VMEM((2, nq, HALF // 2, HALF), F32),
            pltpu.VMEM((2, nq, HALF // 2, HALF), F32),
            pltpu.VMEM((2, nq, HALF // 2, HALF), F32),
            pltpu.VMEM((2, HALF, HALF), F32),
            pltpu.VMEM((k, HALF), F32),
            pltpu.VMEM((nq, k // seq, HALF), F32),
            dma((nz,)),
            dma((2,)),
            dma((2, 2, nz, SUBS)),
            dma((2, 2, nz, SUBS)),
            dma((2, 2, nz, SUBS)),
            dma((2, 2, nz, SUBS)),
            dma((3,)),
            dma((3,)),
            dma((3, tiles + 2)),
            dma((3, tiles + 2)),
        ],
        compiler_params=pltpu.CompilerParams(
            collective_id=0, has_side_effects=True, vmem_limit_bytes=50 * 1024 * 1024
        ),
    )(tokens, sketch)


def solution(mesh):
    return jax.shard_map(
        functools.partial(shards, dict(mesh.shape)),
        mesh=mesh,
        in_specs=(P("seq", "tp"), P("tp", None)),
        out_specs=(P("seq", None), P("seq", "tp")),
        check_vma=False,
    )
```

```python
import functools
import math

import jax
import jax.numpy as jnp
from jax import lax
from jax.experimental import pallas as pl
from jax.experimental.pallas import tpu as pltpu
from jax.sharding import PartitionSpec as P

MESH = pl.DeviceIdType.MESH
HIGHEST = lax.Precision.HIGHEST
F32 = jnp.float32
BF16 = jnp.bfloat16
HALF = 128
PANEL = 16
SUBS = 1


def dot32(a, b, dims):
    return lax.dot_general(a, b, (dims, ((), ())), precision=HIGHEST, preferred_element_type=F32)


def nn(a, b):
    return dot32(a, b, ((1,), (0,)))


def nt(a, b):
    return dot32(a, b, ((1,), (1,)))


def tn(a, b):
    return dot32(a, b, ((0,), (0,)))


def split_parts(value):
    high = value.astype(BF16)
    low = (value - high.astype(F32)).astype(BF16)
    return high, low


def inverse_factor(matrix):
    size = matrix.shape[0]
    sub = lax.broadcasted_iota(jnp.int32, (PANEL, HALF), 0)
    lane = lax.broadcasted_iota(jnp.int32, (PANEL, HALF), 1)
    rest = matrix
    done = []
    for first in range(0, size, PANEL):
        panel = rest[:PANEL]
        below = rest[PANEL:]
        columns = [
            jnp.broadcast_to(panel[:, first + j : first + j + 1], (PANEL, HALF)) for j in range(PANEL)
        ]
        inside = (lane >= first) & (lane < first + PANEL)
        panel = jnp.where(inside, jnp.where(lane - first == sub, 1.0, 0.0), panel)
        work = columns + [panel]
        kept = jnp.zeros((PANEL, HALF), F32)
        pivots = jnp.ones((PANEL, HALF), F32)
        for j in range(PANEL):
            here = sub == j
            rows = [jnp.broadcast_to(item[j : j + 1], (PANEL, HALF)) for item in work]
            pivot = rows[0]
            inverse = 1.0 / work[0]
            scale = jnp.broadcast_to(inverse[j : j + 1], (PANEL, HALF))
            factor = jnp.where(here, -1.0, work[0]) * scale
            kept = jnp.where(here, rows[-1], kept)
            pivots = jnp.where(here, pivot, pivots)
            work = [
                jnp.where(here, 0.0, item) - factor * row for item, row in zip(work[1:], rows[1:])
            ]
        scaled = kept * lax.rsqrt(pivots)
        done.append(jnp.where(lane <= sub + first, scaled, 0.0))
        if first + PANEL < size:
            solved = work[0]
            count = size - first - PANEL
            pieces = []
            for begin, end in ((0, PANEL), (PANEL, count)):
                if begin >= end:
                    continue
                low = below[begin:end]
                low_lane = lax.broadcasted_iota(jnp.int32, (end - begin, HALF), 1)
                update = jnp.where((low_lane >= first) & (low_lane < first + PANEL), 0.0, low)
                terms = [low[:, first + j : first + j + 1] * solved[j : j + 1] for j in range(PANEL)]
                while len(terms) > 1:
                    terms = [a + b for a, b in zip(terms[::2], terms[1::2])]
                pieces.append(update - terms[0])
            rest = jnp.concatenate(pieces, axis=0) if len(pieces) > 1 else pieces[0]
        yield None
    return jnp.concatenate(done, axis=0)


def kernel(
    nq, nz, total,
    tok_hbm, sk_hbm, basis_out, coef_out,
    tok, sk, weights, part, ring, s_all,
    gsrc, ga, gb, gfull,
    c0, cx, cp, cr, cg, outs, landed,
    tok_sem, sk_sem, rs_send, rs_recv, ag_send, ag_recv, g_send, g_recv,
    c_send, c_recv,
):
    rows, feats = tok.shape
    chunk = rows // nz
    unit = chunk // 2
    piece_rows = unit // SUBS
    dist = nz // 2
    me = lax.axis_index("seq")
    z = lax.axis_index("tp")
    q, core = me // 2, lax.rem(me, 2)
    other = q * 2 + (1 - core)
    up, down = lax.rem(z + 1, nz), lax.rem(z + nz - 1, nz)
    seq_count = nq * 2

    def remote(src, dst, send, recv, seq_id, z_id):
        return pltpu.make_async_remote_copy(
            src_ref=src, dst_ref=dst, send_sem=send, recv_sem=recv,
            device_id=(seq_id, z_id), device_id_type=MESH,
        )

    def xy_peer(o):
        peer = lax.rem(q + o, nq)
        return peer, peer * 2 + core

    def seq_peer(o):
        return lax.rem(me + o, seq_count)

    def chunk_of(j):
        return lax.rem(z + j, nz)

    sk_copies = [
        pltpu.make_async_copy(sk_hbm.at[:, pl.ds(h * HALF, HALF)], sk.at[h], sk_sem.at[h])
        for h in range(2)
    ]
    tok_copies = {}
    order = [dist]
    for s in range(1, dist):
        order += [dist - s, nz - dist + s]
    order.append(0)
    for j in order:
        at = pl.ds(pl.multiple_of(chunk_of(j) * chunk, chunk), chunk)
        tok_copies[j] = pltpu.make_async_copy(tok_hbm.at[at], tok.at[at], tok_sem.at[j])
    sk_copies[0].start()
    tok_copies[order[0]].start()

    barrier = pltpu.get_barrier_semaphore()

    def greet_seq(o, carry):
        pl.semaphore_signal(barrier, inc=1, device_id=(seq_peer(o), z), device_id_type=MESH)
        return carry

    def greet_z(o, carry):
        pl.semaphore_signal(
            barrier, inc=1, device_id=(me, lax.rem(z + o, nz)), device_id_type=MESH
        )
        return carry

    lax.fori_loop(1, nz, greet_z, 0)
    lax.fori_loop(1, seq_count, greet_seq, 0)

    tok_copies[order[0]].wait()
    loaded = {order[0]}
    sk_copies[1].start()
    for j in order[1:]:
        tok_copies[j].start()

    def prepare_weights(h):
        sk_copies[h].wait()
        step = min(256, feats)

        @pl.loop(0, feats // step)
        def _(i):
            at = pl.ds(pl.multiple_of(i * step, step), step)
            high, low = split_parts(sk[h, at, :])
            weights[h, at, :HALF] = high
            weights[h, at, HALF:] = low

    def compute_part(h, j):
        if j not in loaded:
            tok_copies[j].wait()
            loaded.add(j)
        at = pl.ds(pl.multiple_of(chunk_of(j) * chunk, chunk), chunk)
        both = jnp.dot(tok[at, :], weights[h], preferred_element_type=F32)
        part[h, j] = both[:, :HALF] + both[:, HALF:]

    def part_rows(u, b):
        return pl.ds(u * unit + b * piece_rows, piece_rows)

    sent = []

    def rs_copy(h, d, s, u, b, src):
        slot = s * 2 + u
        return remote(
            src, ring.at[h, d, slot, b], rs_send.at[h, d, slot, b], rs_recv.at[h, d, slot, b],
            me, up if d == 0 else down,
        )

    def rs_send_unit(h, d, s, u, b, src):
        copy = rs_copy(h, d, s, u, b, src)
        copy.start()
        sent.append(copy)

    def rs_wait(h, d, s, u, b):
        rs_copy(h, d, s, u, b, ring.at[h, d, s * 2 + u, b]).wait_recv()

    def own_chunk(h):
        at = pl.multiple_of(z * chunk, chunk)
        slot = (dist - 1) * 2
        for u in range(2):
            for b in range(SUBS):
                for d in range(2):
                    rs_wait(h, d, dist - 1, u, b)
                value = part[h, 0, part_rows(u, b), :]
                value = value + ring[h, 0, slot + u, b] + ring[h, 1, slot + u, b]
                s_all[h, pl.ds(at + u * unit + b * piece_rows, piece_rows), :] = value

    def ag_unit(h, d, k, u, b, c):
        start = c * chunk + u * unit + b * piece_rows
        at = pl.ds(pl.multiple_of(start, piece_rows), piece_rows)
        slot = k * 2 + u
        return remote(
            s_all.at[h, at], s_all.at[h, at], ag_send.at[h, d, slot, b], ag_recv.at[h, d, slot, b],
            me, up if d == 0 else down,
        )

    def ag_copy(h, d, k, u, b):
        c = lax.rem(z + nz - k, nz) if d == 0 else lax.rem(z + k, nz)
        return ag_unit(h, d, k, u, b, c)

    def ag_arrived(h, d, k, u, b):
        c = lax.rem(z + nz - k - 1, nz) if d == 0 else lax.rem(z + k + 1, nz)
        ag_unit(h, d, k, u, b, c).wait_recv()

    if dist == 4:
        turns = [
            (0, 0, 1, 0), (0, 0, 0, 1), (0, 1, 1, 0), (0, 0, 1, 1), (0, 0, 0, 2), (0, 1, 1, 1),
            (0, 0, 1, 2), (0, 0, 0, 3), (0, 1, 0, 1), (0, 0, 1, 3), (0, 1, 1, 2), (0, 1, 0, 2),
            (1, 0, 1, 0), (0, 1, 1, 3), (0, 1, 0, 3), (1, 0, 0, 0), (1, 0, 1, 1), (1, 1, 1, 0),
            (1, 0, 0, 1), (1, 0, 1, 2), (1, 1, 0, 0), (1, 0, 0, 2), (1, 0, 1, 3), (1, 1, 1, 1),
            (1, 1, 0, 1), (1, 1, 1, 2), (1, 1, 0, 2), (1, 1, 1, 3),
        ]
    else:
        turns = [(0, h, x, k) for k in range(dist) for h in range(2) for x in (1, 0) if k or x]
        turns += [
            (1, h, x, k) for k in range(dist) for h in range(2) for x in (1, 0) if k < dist - 1 or x
        ]

    def places(k):
        return dist - k, (nz - dist + k) % nz

    have = set()

    def ensure(h, j):
        if (h, j) not in have:
            if not any(half == h for half, _ in have):
                prepare_weights(h)
            compute_part(h, j)
            have.add((h, j))

    def ring_turn(i):
        gather, h, long, k = turns[i]
        if not gather:
            for j in places(k):
                ensure(h, j)
            if i == 0:
                pl.semaphore_wait(barrier, seq_count - 1 + nz - 1)
        for b in range(SUBS):
            for d in range(2):
                u = d if long else 1 - d
                if gather:
                    if k > 0:
                        ag_arrived(h, d, k - 1, u, b)
                    copy = ag_copy(h, d, k, u, b)
                    copy.start()
                    sent.append(copy)
                    continue
                j = places(k)[d]
                if k == (0 if long else 1):
                    rs_send_unit(h, d, k, u, b, part.at[h, j, part_rows(u, b)])
                else:
                    rs_wait(h, d, k - 1, u, b)
                    slot = (k - 1) * 2 + u
                    ring[h, d, slot, b] = ring[h, d, slot, b] + part[h, j, part_rows(u, b), :]
                    rs_send_unit(h, d, k, u, b, ring.at[h, d, slot, b])
        for ahead in turns[i + 1 : i + 3]:
            if not ahead[0]:
                for j in places(ahead[3]):
                    ensure(ahead[1], j)

    progress = []

    def ring_to(count):
        while len(progress) < count:
            ring_turn(len(progress))
            progress.append(1)

    def gather_last(h, long):
        for b in range(SUBS):
            for d in range(2):
                if long:
                    ag_arrived(h, d, dist - 1, d, b)
                else:
                    ag_arrived(h, d, dist - 2, 1 - d, b)

    def probe_of(sized, step):
        return remote(sized, sized, g_send.at[step], g_recv.at[step], me, up)

    def gram_sum():
        piece = gsrc.shape[0] // seq_count

        def rows_of(i):
            return pl.ds(pl.multiple_of(i * piece, piece), piece)

        def first(o, carry):
            peer = seq_peer(o)
            remote(
                gsrc.at[rows_of(peer)], ga.at[me], g_send.at[0], g_recv.at[0], peer, z
            ).start()
            return carry

        lax.fori_loop(1, seq_count, first, 0)
        ga[me] = gsrc[rows_of(me), :]
        yield
        probe = probe_of(ga.at[pl.ds(0, seq_count - 1)], 0)
        probe.wait_recv()
        value = ga[0]
        for i in range(1, seq_count):
            value = value + ga[i]
        gb[z] = value

        def second(o, carry):
            remote(
                gb.at[z], gb.at[z], g_send.at[1], g_recv.at[1], me, lax.rem(z + o, nz)
            ).start()
            return carry

        lax.fori_loop(1, nz, second, 0)
        probe.wait_send()
        yield
        probe = probe_of(gb.at[pl.ds(0, nz - 1)], 1)
        probe.wait_recv()
        value = gb[0]
        for i in range(1, nz):
            value = value + gb[i]
        gfull[rows_of(me), :] = value

        def third(o, carry):
            remote(
                gfull.at[rows_of(me)], gfull.at[rows_of(me)], g_send.at[2], g_recv.at[2],
                seq_peer(o), z,
            ).start()
            return carry

        lax.fori_loop(1, seq_count, third, 0)
        probe.wait_send()
        yield
        probe = probe_of(gfull.at[pl.ds(0, (seq_count - 1) * piece)], 2)
        probe.wait_recv()
        probe.wait_send()
        yield

    tile = min(512, feats)
    per_tile = tile // HALF

    def product(h, j, first, after_tile=None):
        at = pl.ds(pl.multiple_of(chunk_of(j) * chunk, chunk), chunk)
        high, low = split_parts(s_all[h, at, :].T)
        left = jnp.concatenate([high, low], axis=0)
        for t in range(feats // tile):
            both = jnp.dot(left, tok[at, t * tile : (t + 1) * tile], preferred_element_type=F32)
            value = both[:HALF] + both[HALF:]
            for i in range(per_tile):
                item = value[:, i * HALF : (i + 1) * HALF]
                p = t * per_tile + i
                c0[h, p] = item if first else c0[h, p] + item
            if after_tile is not None:
                after_tile(t)

    split = HALF // 2

    def core_copy(h, t):
        give = pl.ds(pl.multiple_of((1 - core) * split, split), split)
        at = pl.ds(t * per_tile, per_tile)
        return remote(
            c0.at[h, at, give], cx.at[h, at], c_send.at[h, t], c_recv.at[h, t], other, z
        )

    tiles = feats // tile

    def start_core(h):
        def after(t):
            copy = core_copy(h, t)
            copy.start()
            sent.append(copy)

        return after

    def coef_sum(h):
        keep = pl.ds(pl.multiple_of(core * split, split), split)
        for t in range(tiles):
            core_copy(h, t).wait_recv()
            for i in range(per_tile):
                p = t * per_tile + i
                cp[h, p] = c0[h, p, keep, :] + cx[h, p]

                @pl.when(p != q)
                def _(p=p):
                    remote(
                        cp.at[h, p], cr.at[h, q], c_send.at[h, tiles], c_recv.at[h, tiles],
                        p * 2 + core, z,
                    ).start()

        cr[h, q] = cp[h, q]
        yield
        sized = cr.at[h, pl.ds(0, nq - 1)]
        probe = remote(sized, sized, c_send.at[h, tiles], c_recv.at[h, tiles], me, up)
        probe.wait_recv()
        probe.wait_send()
        value = cr[h, 0]
        for i in range(1, nq):
            value = value + cr[h, i]
        cg[h, keep, :] = value
        copy = remote(
            cg.at[h, keep], cg.at[h, keep], c_send.at[h, tiles + 1], c_recv.at[h, tiles + 1],
            other, z,
        )
        copy.start()
        yield
        copy.wait()
        yield

    def run(gen, steps=None):
        count = 0
        while steps is None or count < steps:
            try:
                next(gen)
            except StopIteration as stop:
                return stop.value
            count += 1
        return None

    coef = [coef_sum(h) for h in range(2)]
    own = pl.ds(pl.multiple_of(z * chunk, chunk), chunk)
    def pair(h, k):
        product(h, nz - k, False)
        product(h, k, False)

    full = dist == 4
    ring_to(12 if full else len(turns) // 2)
    ensure(0, 0)
    own_chunk(0)
    ring_to(15 if full else 0)
    own0 = s_all[0, own, :]
    gsrc[:HALF] = tn(own0, own0)
    gsrc[3 * HALF :] = jnp.zeros((HALF, HALF), F32)
    ensure(1, 0)
    ring_to(17 if full else 0)
    own_chunk(1)
    ring_to(18 if full else 0)
    own1 = s_all[1, own, :]
    gsrc[HALF : 2 * HALF] = tn(own1, s_all[0, own, :])
    gsrc[2 * HALF : 3 * HALF] = tn(own1, own1)
    gram = gram_sum()
    run(gram, 1)
    ring_to(19 if full else 0)
    product(0, 0, True)
    product(1, 0, True)
    if full:
        ring_to(20)
        pair(0, 1)
        ring_to(22)
        run(gram, 1)
        ring_to(23)
        pair(0, 2)
        ring_to(24)
        gather_last(0, 0)
        pair(0, 3)
        ring_to(25)
        gather_last(0, 1)
        product(0, 4, False, start_core(0))
        ring_to(26)
        run(gram, 1)
        run(coef[0], 1)
        pair(1, 1)
        ring_to(27)
        pair(1, 2)
        ring_to(28)
        gather_last(1, 0)
        pair(1, 3)
        gather_last(1, 1)
        product(1, 4, False, start_core(1))
    else:
        ring_to(len(turns))
        run(gram, 2)
        for h in range(2):
            gather_last(h, 0)
            gather_last(h, 1)
            for j in order[:-1]:
                product(h, j, False, start_core(h) if j == order[-2] else None)
        run(coef[0], 1)
    run(coef[1], 1)
    run(gram, 1)
    chol0 = inverse_factor(gfull[:HALF])
    w00 = run(chol0)
    run(coef[0], 1)
    low10 = nt(gfull[HALF : 2 * HALF], w00)
    chol1 = inverse_factor(gfull[2 * HALF : 3 * HALF] - nt(low10, low10))
    mixed = nn(low10, w00)
    w11 = run(chol1)
    w10 = -nn(w11, mixed)
    root = math.sqrt(total)
    step = min(256, rows)

    def make_basis():
        upper = jnp.concatenate([w00, jnp.zeros((HALF, HALF), F32)], axis=1)
        factor = jnp.concatenate([upper, jnp.concatenate([w10, w11], axis=1)], axis=0) * root

        @pl.loop(0, rows // step)
        def _(i):
            at = pl.ds(pl.multiple_of(i * step, step), step)
            left = jnp.concatenate([s_all[0, at, :], s_all[1, at, :]], axis=1)
            basis_out[at, :] = nt(left, factor)

    block = 2 * HALF // seq_count

    def rows_for(seq_id):
        return pl.ds(pl.multiple_of(seq_id * block, block), block)

    def deliver(first, count):
        def body(p, carry):
            @pl.when(p != q)
            def _():
                seq_id = p * 2 + core
                remote(
                    outs.at[rows_for(seq_id)], landed.at[q], c_send.at[2, 0], c_recv.at[2, 0],
                    seq_id, z,
                ).start()

            return carry

        lax.fori_loop(first, first + count, body, 0)

    run(coef[0])
    reduced0 = cg[0]
    outs[:HALF] = nn(w00, reduced0) / root
    deliver(0, nq // 2)
    early = nn(w10, reduced0)
    run(coef[1])
    outs[HALF:] = (early + nn(w11, cg[1])) / root
    deliver(nq // 2, nq // 2)
    landed[q] = outs[rows_for(me), :]
    for copy in sent:
        copy.wait_send()

    make_basis()
    sized = landed.at[pl.ds(0, nq - 1)]
    probe = remote(sized, sized, c_send.at[2, 0], c_recv.at[2, 0], me, up)
    probe.wait_recv()
    probe.wait_send()
    for i in range(nq):
        coef_out[:, i * HALF : (i + 1) * HALF] = landed[i]


def shards(mesh_shape, tokens, sketch):
    rows, feats = tokens.shape
    seq, nz = mesh_shape["seq"], mesh_shape["tp"]
    nq = seq // 2
    total = rows * seq
    chunk = rows // nz
    unit = chunk // 2
    dist = nz // 2
    k = 2 * HALF
    dma = pltpu.SemaphoreType.DMA
    tiles = feats // min(512, feats)
    return pl.pallas_call(
        functools.partial(kernel, nq, nz, total),
        out_shape=(
            jax.ShapeDtypeStruct((rows, k), F32),
            jax.ShapeDtypeStruct((k // seq, feats), F32),
        ),
        in_specs=[pl.BlockSpec(memory_space=pl.ANY)] * 2,
        out_specs=(pl.BlockSpec(memory_space=pltpu.VMEM),) * 2,
        scratch_shapes=[
            pltpu.VMEM((rows, feats), BF16),
            pltpu.VMEM((2, feats, HALF), F32),
            pltpu.VMEM((2, feats, k), BF16),
            pltpu.VMEM((2, nz, chunk, HALF), F32),
            pltpu.VMEM((2, 2, nz, SUBS, unit // SUBS, HALF), F32),
            pltpu.VMEM((2, rows, HALF), F32),
            pltpu.VMEM((4 * HALF, HALF), F32),
            pltpu.VMEM((seq, 4 * HALF // seq, HALF), F32),
            pltpu.VMEM((nz, 4 * HALF // seq, HALF), F32),
            pltpu.VMEM((4 * HALF, HALF), F32),
            pltpu.VMEM((2, nq, HALF, HALF), F32),
            pltpu.VMEM((2, nq, HALF // 2, HALF), F32),
            pltpu.VMEM((2, nq, HALF // 2, HALF), F32),
            pltpu.VMEM((2, nq, HALF // 2, HALF), F32),
            pltpu.VMEM((2, HALF, HALF), F32),
            pltpu.VMEM((k, HALF), F32),
            pltpu.VMEM((nq, k // seq, HALF), F32),
            dma((nz,)),
            dma((2,)),
            dma((2, 2, nz, SUBS)),
            dma((2, 2, nz, SUBS)),
            dma((2, 2, nz, SUBS)),
            dma((2, 2, nz, SUBS)),
            dma((3,)),
            dma((3,)),
            dma((3, tiles + 2)),
            dma((3, tiles + 2)),
        ],
        compiler_params=pltpu.CompilerParams(
            collective_id=0, has_side_effects=True, vmem_limit_bytes=50 * 1024 * 1024
        ),
    )(tokens, sketch)


def solution(mesh):
    return jax.shard_map(
        functools.partial(shards, dict(mesh.shape)),
        mesh=mesh,
        in_specs=(P("seq", "tp"), P("tp", None)),
        out_specs=(P("seq", None), P("seq", "tp")),
        check_vma=False,
    )
```
